768 devices in a mesh: aux: 12 (over z), pair: 64 (over x, y, core).
Axes of the slice: x: 4, y: 8, z: 12, core: 2. Of those that a mesh axis runs over, the one named last changes fastest.
Arguments:
- integrals: bfloat16 [1152, 393216], P('aux', 'pair'), may hold values from -6 to 6
- tile_mask: int32 [12, 6144], P('aux', 'pair'), may hold values 0 or 1
- metric: bfloat16 [1152, 1152], P('pair'), may hold values from -0.0048828125 to 0.0048828125
- owners: int32 [6144], P('pair'), may hold values from 0 to 767
Outputs:
- owner_sums: float32 [768, 64], P(('aux', 'pair'))
The draws below stay inside these ranges and needn't reach their ends.
Inputs may be any that keep to these rules, and one draw needn't show every extreme that they name: `owners`: a device is numbered aux index times 64 plus pair index.
All inputs are finite; a program needn't handle non-finite values. No bound on the sum of `tile_mask` on one device may be relied on, other than what follows from the above.
Results may differ from the reference program's by a relative error of at most 0.0003.
Values may be sent and summed in bfloat16 or wider, within the bound.
A program may use at most 32 MiB of HBM per device.

```python
import math
import jax
import jax.numpy as jnp
import numpy as np
from jax import lax

AUXD = 96
TILES_DEV = 8
TILE = 64
NAUX = 1152
NTILES = 6144
N_AUX = 12
N_PAIR = 64


def plant(values, stream_key, smallest, largest):
    shape = values.shape
    spot = [jax.random.randint(jax.random.fold_in(stream_key, axis), (), 0, shape[axis]) for axis in range(len(shape))]
    values = values.at[tuple(spot)].set(smallest)
    longest = shape.index(max(shape))
    spot[longest] = (spot[longest] + 1) % shape[longest]
    return values.at[tuple(spot)].set(largest)


def steps_of(stream_key, dims, split, smallest, high):
    def one(dim, parts):
        draws = jax.random.uniform(jax.random.fold_in(jax.random.fold_in(stream_key, 6), dim), (parts,), jnp.float32, smallest / len(split), high / len(split))
        return jnp.repeat(jnp.exp(draws), dims[dim] // parts).reshape((-1,) + (1,) * (len(dims) - dim - 1))

    factor_of = one(*split[0])
    for cut in split[1:]:
        factor_of = factor_of * one(*cut)
    return factor_of


def rank_table(amount, slope):
    portions = [(1 << 20) // math.isqrt(rank ** slope) + 1 for rank in range(1, amount + 1)]
    deviation = 1 + sum(portions) // (1 << 30)
    return np.cumsum(np.array([max(1, weight // deviation) for weight in portions]))


def ranked(rng, shape, amount, lean):
    grid = rank_table(amount, lean)
    lot = jax.random.randint(jax.random.fold_in(rng, 1), shape, 0, int(grid[amount - 1]))
    standing = jnp.searchsorted(jnp.asarray(grid, jnp.int32), lot, side="right")
    return jax.random.permutation(jax.random.fold_in(rng, 2), amount)[standing].astype(jnp.int32)


def centred(key, extent, scale, limit, cuts=(), dtype=jnp.bfloat16):
    factor_of = steps_of(key, extent, cuts, -0.22, 0.18) if cuts else 1.0
    entries = jax.random.normal(key, extent, jnp.float32) * scale * factor_of
    return jnp.minimum(jnp.maximum(entries, -limit), limit).astype(dtype)


def setup_inputs(seed: int = 0) -> dict:
    arg_keys = jax.random.split(jax.random.key(seed), 5)
    integrals = centred(arg_keys[0], (NAUX, NTILES * TILE), 1.0, 6.0, ((0, 12), (1, 64)))
    tile_mask = plant((jax.random.randint(arg_keys[1], (N_AUX, NTILES), 0, 3) < 2).astype(jnp.int32), jax.random.fold_in(arg_keys[1], 1), 0, 1)
    metric = centred(arg_keys[2], (NAUX, NAUX), (NAUX * NAUX) ** -0.5, 0.0048828125, ((0, 64),))
    owners = plant(ranked(arg_keys[3], (NTILES,), N_AUX * N_PAIR, 1), jax.random.fold_in(arg_keys[3], 3), 0, (N_AUX * N_PAIR) - 1).astype(jnp.int32)
    return dict(integrals=integrals, tile_mask=tile_mask, metric=metric, owners=owners)


def reference(integrals, tile_mask, metric, owners):
    keep = jnp.repeat(tile_mask, AUXD, axis=0).astype(jnp.bfloat16)
    blocks = integrals.reshape(NAUX, NTILES, TILE) * keep[:, :, None]
    grouped = blocks.reshape(NAUX, N_PAIR, N_AUX * TILES_DEV * TILE).transpose(1, 0, 2)

    def weigh(columns):
        image = jnp.dot(metric, columns, preferred_element_type=jnp.float32)
        return jnp.sum(columns.astype(jnp.float32) * image, axis=0)

    pair_terms = lax.map(weigh, grouped).reshape(NTILES, TILE)
    return jax.ops.segment_sum(pair_terms, owners, num_segments=N_AUX * N_PAIR)
```

```python
import functools

import jax
import jax.numpy as jnp
from jax import lax
from jax.experimental import pallas as pl
from jax.experimental.pallas import tpu as pltpu
from jax.sharding import PartitionSpec as P

MESH = pl.DeviceIdType.MESH
F32, BF16, I32 = jnp.float32, jnp.bfloat16, jnp.int32
NZ, NX, NY = 12, 4, 8
AUXD, WIDTH, NAUX = 96, 512, 1152
CHUNKS = 2
CW = WIDTH // CHUNKS
LANES = 128
SHARD = 18
MAIN = 16
PACKED = NAUX + 2 * LANES
QB = 192
ORDER = (6, 5, 7, 4, 8, 3, 9, 2, 10, 1, 11)


def iota(shape, axis):
    return lax.broadcasted_iota(I32, shape, axis)


def kernel(
    x_hbm, mask_hbm, met_hbm, own_hbm, out_ref,
    src, got, mask, met, own, slots, dense, hits, terms, heard, part, got_y, fold, got_x,
    in_sem, z_send, z_recv, y_send, y_recv, x_send, x_recv, c_send, c_recv,
    t_send, t_recv, p_send, p_recv, q_send, q_recv,
):
    z = lax.axis_index("aux")
    pair = lax.axis_index("pair")
    c = lax.rem(pair, 2)
    y = lax.rem(pair // 2, NY)
    x = pair // (2 * NY)
    r = x * 2 + c

    def at_z(k):
        return lax.rem(z + k, NZ)

    def at_y(k):
        return lax.rem(y + k, NY)

    def at_r(k):
        return lax.rem(r + k, 2 * NX)

    def dev_z(k):
        return {"aux": at_z(k)}

    def dev_y(k):
        return {"pair": (x * NY + at_y(k)) * 2 + c}

    def dev_r(k):
        other = at_r(k)
        return {"pair": ((other // 2) * NY + y) * 2 + lax.rem(other, 2)}

    def dev_x(k):
        return {"pair": (lax.rem(x + k, NX) * NY + y) * 2 + c}

    dev_c = {"pair": (x * NY + y) * 2 + (1 - c)}

    barrier = pltpu.get_barrier_semaphore()
    peers = [dev_z(k) for k in range(1, NZ)] + [dev_y(k) for k in range(1, NY)] + [dev_r(k) for k in range(1, 2 * NX)]
    for peer in peers:
        pl.semaphore_signal(barrier, inc=1, device_id=peer, device_id_type=MESH)

    met_in = pltpu.make_async_copy(met_hbm, met, in_sem.at[NZ])
    mask_in = pltpu.make_async_copy(mask_hbm, mask, in_sem.at[NZ + 1])
    own_in = pltpu.make_async_copy(own_hbm, own, in_sem.at[NZ + 2])
    mask_in.start()
    met_in.start()
    loads = {}
    for k in ORDER + (0,):
        block = at_z(k)
        loads[k] = [
            pltpu.make_async_copy(
                x_hbm.at[:, pl.ds(pl.multiple_of(block * WIDTH + j * CW, LANES), CW)], src.at[block, j], in_sem.at[k]
            )
            for j in range(CHUNKS)
        ]
        for load in loads[k]:
            load.start()
    own_in.start()

    met_in.wait()
    rows = met[...].astype(F32)
    tail = rows[MAIN:SHARD]
    rest = jnp.concatenate([tail[:, i * LANES : (i + 1) * LANES] for i in range(8)], axis=0)
    last = jnp.concatenate([tail[:, 8 * LANES :], jnp.zeros((MAIN - 2, LANES), F32)], axis=0)
    slots[c, x, y] = jnp.concatenate([rows[:MAIN], rest, last], axis=1).astype(BF16)

    mask_in.wait()
    left_half = iota((1, LANES), 1) < 64

    def masked(k):
        block = at_z(k)
        for load in loads[k]:
            load.wait()
        for j in range(CHUNKS):
            for lane in range(CW // LANES):
                tile = block * 8 + (j * CW + lane * LANES) // 64
                keep = jnp.where(left_half, mask[0, tile], mask[0, tile + 1]).astype(F32).astype(BF16)
                cols = pl.ds(lane * LANES, LANES)
                if k == 0:
                    got[j, block, :, cols] = src[block, j, :, cols] * keep
                else:
                    src[block, j, :, cols] = src[block, j, :, cols] * keep

    for k in ORDER:
        masked(k)

    pl.semaphore_wait(barrier, len(peers))

    def remote(s, d, ss, rs, dev):
        return pltpu.make_async_remote_copy(src_ref=s, dst_ref=d, send_sem=ss, recv_sem=rs, device_id=dev, device_id_type=MESH)

    y_copies = [remote(slots.at[c, x, y], slots.at[c, x, y], y_send.at[k], y_recv.at[k], dev_y(k)) for k in range(1, NY)]
    for copy in y_copies:
        copy.start()
    z_copies = [
        [remote(src.at[at_z(k), j], got.at[j, z], z_send.at[j, k], z_recv.at[j, k], dev_z(k)) for k in ORDER]
        for j in range(CHUNKS)
    ]
    for group in z_copies:
        for copy in group:
            copy.start()
    masked(0)

    own_in.wait()
    s = iota((64, 96), 0)
    target = z * 64 + (((s & 7) >> 1) * NY + (s >> 3)) * 2 + (s & 1)
    hit = jnp.where(own[...] == target, 1.0, 0.0).astype(BF16)
    q = iota((96, 96), 1)
    t = iota((96, 96), 0)
    for j in range(CHUNKS):
        for par in range(2):
            wanted = (q >> 3) * 8 + 2 * (j * (CW // LANES) + (q & 7)) + par
            perm = jnp.where((t == wanted) & ((q & 7) < CW // LANES), 1.0, 0.0).astype(BF16)
            hits[j, pl.ds(par * 64, 64), :] = jnp.dot(hit, perm, preferred_element_type=F32).astype(BF16)

    def from_y(k):
        there = lax.rem(y + NY - k, NY)
        return remote(slots.at[c, x, there], slots.at[c, x, there], y_send.at[k], y_recv.at[k], dev_y(k))

    for k in range(1, NY):
        from_y(k).wait_recv()
    x_copies = [remote(slots.at[c, x], slots.at[c, x], x_send.at[k], x_recv.at[k], dev_x(k)) for k in range(1, NX)]
    for copy in x_copies:
        copy.start()
    for k in range(1, NX):
        there = lax.rem(x + NX - k, NX)
        remote(slots.at[c, there], slots.at[c, there], x_send.at[k], x_recv.at[k], dev_x(k)).wait_recv()
    c_copy = remote(slots.at[c], slots.at[c], c_send, c_recv, dev_c)
    c_copy.start()
    remote(slots.at[1 - c], slots.at[1 - c], c_send, c_recv, dev_c).wait_recv()

    def picks(index):
        row = iota((288, 256), 0)
        col = iota((288, 256), 1)
        yy = jnp.zeros_like(row)
        for step in range(1, NY):
            yy = yy + (row >= 36 * step).astype(I32)
        row = row - 36 * yy
        cc = (row >= SHARD).astype(I32)
        row = row - SHARD * cc
        base = cc * 128 + yy * MAIN
        if index is None:
            return jnp.where((row < MAIN) & (col == base + row), 1.0, 0.0).astype(BF16)
        return jnp.where((row >= MAIN) & (col == base + 2 * index + row - MAIN), 1.0, 0.0).astype(BF16)

    main_pick = picks(None)
    for piece in range(9):
        rest_pick = picks(piece % 8)
        cols = pl.ds(piece * LANES, LANES)
        rest_cols = pl.ds(NAUX + (piece // 8) * LANES, LANES)

        @pl.loop(0, NX)
        def _(xx):
            main = slots[:, xx, :, :, cols].reshape(256, LANES)
            extra = slots[:, xx, :, :, rest_cols].reshape(256, LANES)
            both = jnp.dot(main_pick, main, preferred_element_type=F32) + jnp.dot(rest_pick, extra, preferred_element_type=F32)
            dense[pl.ds(pl.multiple_of(xx * 288, 32), 288), cols] = both.astype(BF16)

    def chunk(j):
        for k in ORDER:
            there = lax.rem(z + NZ - k, NZ)
            remote(src.at[there, j], got.at[j, there], z_send.at[j, k], z_recv.at[j, k], dev_z(k)).wait_recv()
        block = got[j].reshape(NAUX, CW)
        acc = jnp.zeros((1, CW), F32)
        for i in range(NAUX // QB):
            image = jnp.dot(dense[pl.ds(i * QB, QB), :], block, preferred_element_type=F32)
            acc = acc + jnp.sum(block[i * QB : (i + 1) * QB].astype(F32) * image, axis=0, keepdims=True)
        pieces = [acc[:, i * LANES : (i + 1) * LANES] for i in range(CW // LANES)]
        terms[j] = jnp.concatenate(pieces + [jnp.zeros((8 - len(pieces), LANES), F32)], axis=0)
        heard[j, z] = terms[j]
        copies = [remote(terms.at[j], heard.at[j, z], t_send.at[j, k], t_recv.at[j, k], dev_z(k)) for k in range(1, NZ)]
        for copy in copies:
            copy.start()
        return copies

    def owned(j):
        for k in range(1, NZ):
            there = lax.rem(z + NZ - k, NZ)
            remote(terms.at[j], heard.at[j, there], t_send.at[j, k], t_recv.at[j, k], dev_z(k)).wait_recv()
        value = heard[j].reshape(96, LANES)
        first = value.astype(BF16)
        value = value - first.astype(F32)
        second = value.astype(BF16)
        third = (value - second.astype(F32)).astype(BF16)
        sums = [jnp.dot(hits[j], v, preferred_element_type=F32) for v in (third, second, first)]
        both = sums[0] + sums[1] + sums[2]
        return both[:64, :64] + both[64:, 64:]

    t_copies = [chunk(0)]
    total = None
    for j in range(1, CHUNKS):
        t_copies.append(chunk(j))
        mine = owned(j - 1)
        total = mine if total is None else total + mine
    mine = owned(CHUNKS - 1)
    total = mine if total is None else total + mine

    part[:, :, :64] = total.reshape(NY, 8, 64)
    part[:, :, 64:] = jnp.zeros((NY, 8, 64), F32)
    p_copies = [remote(part.at[at_y(k)], got_y.at[y], p_send.at[k], p_recv.at[k], dev_y(k)) for k in range(1, NY)]
    for copy in p_copies:
        copy.start()
    got_y[y] = part[y]
    for k in range(1, NY):
        there = lax.rem(y + NY - k, NY)
        remote(part.at[there], got_y.at[there], p_send.at[k], p_recv.at[k], dev_y(k)).wait_recv()
    fold[...] = jnp.sum(got_y[...], axis=0)
    q_copies = [remote(fold, got_x.at[r], q_send.at[k], q_recv.at[k], dev_r(k)) for k in range(1, 2 * NX)]
    for copy in q_copies:
        copy.start()
    got_x[r] = fold[...]
    for k in range(1, 2 * NX):
        there = lax.rem(r + 2 * NX - k, 2 * NX)
        remote(fold, got_x.at[there], q_send.at[k], q_recv.at[k], dev_r(k)).wait_recv()
    final = jnp.sum(got_x[...], axis=0)
    out_ref[...] = jnp.sum(jnp.where(iota((8, LANES), 0) == r, final, 0.0), axis=0, keepdims=True)[:, :64]

    for group in [y_copies, x_copies, [c_copy], p_copies, q_copies] + z_copies + t_copies:
        for copy in group:
            copy.wait_send()


def body(integrals, tile_mask, metric, owners):
    any_spec = pl.BlockSpec(memory_space=pl.ANY)
    dma = pltpu.SemaphoreType.DMA
    return pl.pallas_call(
        kernel,
        out_shape=jax.ShapeDtypeStruct((1, 64), F32),
        in_specs=[any_spec] * 4,
        out_specs=pl.BlockSpec(memory_space=pltpu.VMEM),
        scratch_shapes=[
            pltpu.VMEM((NZ, CHUNKS, AUXD, CW), BF16),
            pltpu.VMEM((CHUNKS, NZ, AUXD, CW), BF16),
            pltpu.SMEM((1, 96), I32),
            pltpu.VMEM((SHARD, NAUX), BF16),
            pltpu.VMEM((1, 96), I32),
            pltpu.VMEM((2, NX, NY, MAIN, PACKED), BF16),
            pltpu.VMEM((NAUX, NAUX), BF16),
            pltpu.VMEM((CHUNKS, 128, 96), BF16),
            pltpu.VMEM((CHUNKS, 8, LANES), F32),
            pltpu.VMEM((CHUNKS, NZ, 8, LANES), F32),
            pltpu.VMEM((NY, 8, LANES), F32),
            pltpu.VMEM((NY, 8, LANES), F32),
            pltpu.VMEM((8, LANES), F32),
            pltpu.VMEM((2 * NX, 8, LANES), F32),
            dma((NZ + 3,)),
            dma((CHUNKS, NZ)), dma((CHUNKS, NZ)),
            dma((NY,)), dma((NY,)),
            dma((NX,)), dma((NX,)),
            dma, dma,
            dma((CHUNKS, NZ)), dma((CHUNKS, NZ)),
            dma((NY,)), dma((NY,)),
            dma((2 * NX,)), dma((2 * NX,)),
        ],
        compiler_params=pltpu.CompilerParams(collective_id=0, has_side_effects=True, vmem_limit_bytes=40 << 20),
    )(integrals, tile_mask, metric, owners.reshape(1, -1))


def solution(mesh):
    return jax.shard_map(
        body,
        mesh=mesh,
        in_specs=(P("aux", "pair"), P("aux", "pair"), P("pair", None), P("pair")),
        out_specs=P(("aux", "pair"), None),
        check_vma=False,
    )
```

```python
import functools

import jax
import jax.numpy as jnp
from jax import lax
from jax.experimental import pallas as pl
from jax.experimental.pallas import tpu as pltpu
from jax.sharding import PartitionSpec as P

MESH = pl.DeviceIdType.MESH
F32, BF16, I32 = jnp.float32, jnp.bfloat16, jnp.int32
NZ, NX, NY = 12, 4, 8
AUXD, WIDTH, NAUX = 96, 512, 1152
CHUNKS = 2
CW = WIDTH // CHUNKS
LANES = 128
SHARD = 18
MAIN = 16
PACKED = NAUX + 2 * LANES
QB = 192
ORDER = (6, 5, 7, 4, 8, 3, 9, 2, 10, 1, 11)
AROUND = sorted(
    [(i, j) for i in range(NX) for j in range(NY) if i or j], key=lambda k: -min(k[0], NX - k[0]) - min(k[1], NY - k[1])
)


def iota(shape, axis):
    return lax.broadcasted_iota(I32, shape, axis)


def kernel(
    x_hbm, mask_hbm, met_hbm, own_hbm, out_ref,
    got, masks, keep, met, own, slots, dense, hits, terms, heard, part, rows_in,
    in_sem, z_send, z_recv, m_send, m_recv, o_send, o_recv, y_send, y_recv, x_send, x_recv, c_send, c_recv,
    t_send, t_recv, p_send, p_recv,
):
    z = lax.axis_index("aux")
    pair = lax.axis_index("pair")
    c = lax.rem(pair, 2)
    y = lax.rem(pair // 2, NY)
    x = pair // (2 * NY)
    place = x * NY + y

    def at_z(k):
        return lax.rem(z + k, NZ)

    def at_y(k):
        return lax.rem(y + k, NY)

    def dev_z(k):
        return {"aux": at_z(k)}

    def dev_zc(k, flip):
        return {"aux": at_z(k), "pair": place * 2 + (1 - c if flip else c)}

    def dev_y(k):
        return {"pair": (x * NY + at_y(k)) * 2 + c}

    def place_at(k):
        return lax.rem(x + k[0], NX) * NY + lax.rem(y + k[1], NY)

    def dev_xy(k):
        return {"pair": place_at(k) * 2 + c}

    def dev_x(k):
        return {"pair": (lax.rem(x + k, NX) * NY + y) * 2 + c}

    dev_c = {"pair": (x * NY + y) * 2 + (1 - c)}

    def remote(s, d, ss, rs, dev):
        return pltpu.make_async_remote_copy(src_ref=s, dst_ref=d, send_sem=ss, recv_sem=rs, device_id=dev, device_id_type=MESH)

    def columns(block, j):
        return x_hbm.at[:, pl.ds(pl.multiple_of(block * WIDTH + j * CW, LANES), CW)]

    met_in = pltpu.make_async_copy(met_hbm, met, in_sem.at[0])
    met_in.start()
    barrier = pltpu.get_barrier_semaphore()
    peers = [dev_zc(k, False) for k in ORDER] + [dev_xy(k) for k in AROUND] + [dev_zc(k, True) for k in ORDER + (0,)]
    for peer in peers:
        pl.semaphore_signal(barrier, inc=1, device_id=peer, device_id_type=MESH)
    locals_in = [
        pltpu.make_async_copy(mask_hbm, masks.at[z], in_sem.at[1]),
        pltpu.make_async_copy(own_hbm, own.at[c], in_sem.at[2]),
    ] + [pltpu.make_async_copy(columns(z, j), got.at[j, z], in_sem.at[3 + j]) for j in range(CHUNKS)]
    for copy in locals_in:
        copy.start()
    pl.semaphore_wait(barrier, len(peers))

    z_copies = [
        [remote(columns(at_z(k), j), got.at[j, z], z_send.at[j, k], z_recv.at[j, k], dev_z(k)) for k in ORDER]
        for j in range(CHUNKS)
    ]
    m_copies = [remote(mask_hbm, masks.at[z], m_send.at[k], m_recv.at[k], dev_z(k)) for k in ORDER]
    for copy in m_copies + z_copies[0]:
        copy.start()

    met_in.wait()
    rows = met[...].astype(F32)
    tail = rows[MAIN:SHARD]
    rest = jnp.concatenate([tail[:, i * LANES : (i + 1) * LANES] for i in range(8)], axis=0)
    last = jnp.concatenate([tail[:, 8 * LANES :], jnp.zeros((MAIN - 2, LANES), F32)], axis=0)
    slots[c, x, y] = jnp.concatenate([rows[:MAIN], rest, last], axis=1).astype(BF16)
    y_copies = [remote(slots.at[c, x, y], slots.at[c, x, y], y_send.at[k], y_recv.at[k], dev_y(k)) for k in range(1, NY)]
    for copy in y_copies:
        copy.start()
    o_copy = remote(own_hbm, own.at[c], o_send, o_recv, dev_c)
    o_copy.start()
    for group in z_copies[1:]:
        for copy in group:
            copy.start()

    for copy in locals_in:
        copy.wait()
    for k in ORDER:
        there = lax.rem(z + NZ - k, NZ)
        remote(mask_hbm, masks.at[there], m_send.at[k], m_recv.at[k], dev_z(k)).wait_recv()
    spread = jnp.where(iota((96, WIDTH), 0) == z * 8 + (iota((96, WIDTH), 1) >> 6), 1.0, 0.0).astype(BF16)
    entries = jnp.concatenate([masks[a] for a in range(NZ)] + [jnp.zeros((4, 96), I32)], axis=0).astype(F32).astype(BF16)
    keep[...] = jnp.dot(entries, spread, preferred_element_type=F32)

    remote(own_hbm, own.at[1 - c], o_send, o_recv, dev_c).wait_recv()
    target = z * 64 + iota((32, 96), 0) * 2 + c
    q = iota((96, 192), 1)
    t = iota((96, 192), 0)
    for j in range(CHUNKS):
        for par in range(2):
            picked = jnp.zeros((32, 192), F32)
            for core in range(2):
                qq = q - 96 * core
                wanted = (qq >> 3) * 8 + 2 * (j * (CW // LANES) + (qq & 7)) + par
                perm = jnp.where((t == wanted) & ((qq & 7) < CW // LANES) & (qq >= 0) & (qq < 96), 1.0, 0.0).astype(BF16)
                hit = jnp.where(own[core] == target, 1.0, 0.0).astype(BF16)
                picked = picked + jnp.dot(hit, perm, preferred_element_type=F32)
            hits[j, pl.ds(par * 32, 32), :] = picked.astype(BF16)

    def from_y(k):
        there = lax.rem(y + NY - k, NY)
        return remote(slots.at[c, x, there], slots.at[c, x, there], y_send.at[k], y_recv.at[k], dev_y(k))

    for k in range(1, NY):
        from_y(k).wait_recv()
    x_copies = [remote(slots.at[c, x], slots.at[c, x], x_send.at[k], x_recv.at[k], dev_x(k)) for k in (2, 1, 3)]
    for copy in x_copies:
        copy.start()

    def between(k, core):
        there = lax.rem(x + NX - k, NX)
        return remote(slots.at[core, there], slots.at[core, there], c_send.at[k], c_recv.at[k], dev_c)

    row = iota((288, 256), 0)
    col = iota((288, 256), 1)
    yy = jnp.zeros_like(row)
    for step in range(1, NY):
        yy = yy + (row >= 36 * step).astype(I32)
    row = row - 36 * yy
    cc = (row >= SHARD).astype(I32)
    row = row - SHARD * cc
    first_rows = jnp.where((row < MAIN) & (col == cc * 128 + yy * MAIN + row), 1.0, 0.0).astype(BF16)
    last_rows = jnp.where((row >= MAIN) & (col == cc * 16 + yy * 2 + row - MAIN), 1.0, 0.0).astype(BF16)[:, :32]
    row = iota((256, 256), 0)
    col = iota((256, 256), 1)
    slot = (row & 31) >> 1
    regroup = jnp.where(col == slot * MAIN + 2 * (row >> 5) + (row & 1), 1.0, 0.0).astype(BF16)

    def spread_rows(k):
        there = lax.rem(x + NX - k, NX)
        rest = [slots[:, there, :, :, pl.ds(NAUX + i * LANES, LANES)].reshape(256, LANES) for i in range(2)]
        pieces = jnp.dot(regroup, rest[0], preferred_element_type=F32).astype(BF16)
        piece = jnp.dot(regroup[:32], rest[1], preferred_element_type=F32).astype(BF16)
        ends = jnp.concatenate([pieces[32 * i : 32 * (i + 1)] for i in range(8)] + [piece], axis=1)
        for i in range(3):
            cols = pl.ds(i * 384, 384)
            main = slots[:, there, :, :, cols].reshape(256, 384)
            both = jnp.dot(first_rows, main, preferred_element_type=F32)
            both = both + jnp.dot(last_rows, ends[:, i * 384 : (i + 1) * 384], preferred_element_type=F32)
            dense[pl.ds(pl.multiple_of(there * 288, 32), 288), cols] = both.astype(BF16)

    c_copies = [between(k, c) for k in range(NX)]
    c_copies[0].start()
    for k, before in ((1, 0), (3, 1), (2, 3)):
        there = lax.rem(x + NX - k, NX)
        remote(slots.at[c, there], slots.at[c, there], x_send.at[k], x_recv.at[k], dev_x(k)).wait_recv()
        c_copies[k].start()
        between(before, 1 - c).wait_recv()
        spread_rows(before)
    between(2, 1 - c).wait_recv()
    spread_rows(2)

    def chunk(j):
        for k in (0,) + ORDER:
            there = lax.rem(z + NZ - k, NZ)
            if k:
                remote(columns(there, j), got.at[j, there], z_send.at[j, k], z_recv.at[j, k], dev_z(k)).wait_recv()
            got[j, there] = got[j, there] * keep[pl.ds(there, 1), pl.ds(j * CW, CW)].astype(BF16)
        block = got[j].reshape(NAUX, CW)
        acc = jnp.zeros((1, CW), F32)
        for i in range(NAUX // QB):
            image = jnp.dot(dense[pl.ds(i * QB, QB), :], block, preferred_element_type=F32)
            acc = acc + jnp.sum(block[i * QB : (i + 1) * QB].astype(F32) * image, axis=0, keepdims=True)
        pieces = [acc[:, i * LANES : (i + 1) * LANES] for i in range(CW // LANES)]
        terms[j] = jnp.concatenate(pieces + [jnp.zeros((8 - len(pieces), LANES), F32)], axis=0)
        copies = [
            remote(terms.at[j], heard.at[j, c * NZ + z], t_send.at[j, int(flip), k], t_recv.at[j], dev_zc(k, flip))
            for k in ORDER + (0,) for flip in (False, True) if k or flip
        ]
        for copy in copies:
            copy.start()
        heard[j, c * NZ + z] = terms[j]
        return copies

    def owned(j):
        others = heard.at[j, pl.ds(0, 2 * NZ - 1)]
        pltpu.make_async_copy(others, others, t_recv.at[j]).wait()
        value = heard[j].reshape(192, LANES)
        first = value.astype(BF16)
        value = value - first.astype(F32)
        second = value.astype(BF16)
        third = (value - second.astype(F32)).astype(BF16)
        sums = [jnp.dot(hits[j], v, preferred_element_type=F32) for v in (third, second, first)]
        both = sums[0] + sums[1] + sums[2]
        return both[:32, :64] + both[32:, 64:]

    t_copies = [chunk(0)]
    total = None
    for j in range(1, CHUNKS):
        t_copies.append(chunk(j))
        mine = owned(j - 1)
        total = mine if total is None else total + mine
    mine = owned(CHUNKS - 1)
    total = mine if total is None else total + mine

    total = jnp.concatenate([total, jnp.zeros((32, 64), F32)], axis=1)
    for i in range(NX * NY):
        part[i] = total[i : i + 1]
    p_copies = [
        remote(part.at[place_at(k)], rows_in.at[place], p_send.at[i], p_recv, dev_xy(k)) for i, k in enumerate(AROUND)
    ]
    for copy in p_copies:
        copy.start()
    rows_in[place] = part[place]
    others = rows_in.at[pl.ds(0, NX * NY - 1)]
    pltpu.make_async_copy(others, others, p_recv).wait()
    out_ref[...] = jnp.sum(rows_in[...], axis=0)[:, :64]

    for group in [y_copies, x_copies, c_copies, [o_copy], m_copies, p_copies] + z_copies + t_copies:
        for copy in group:
            copy.wait_send()


def body(integrals, tile_mask, metric, owners):
    any_spec = pl.BlockSpec(memory_space=pl.ANY)
    dma = pltpu.SemaphoreType.DMA
    return pl.pallas_call(
        kernel,
        out_shape=jax.ShapeDtypeStruct((1, 64), F32),
        in_specs=[any_spec] * 4,
        out_specs=pl.BlockSpec(memory_space=pltpu.VMEM),
        scratch_shapes=[
            pltpu.VMEM((CHUNKS, NZ, AUXD, CW), BF16),
            pltpu.VMEM((NZ, 1, 96), I32),
            pltpu.VMEM((16, WIDTH), F32),
            pltpu.VMEM((SHARD, NAUX), BF16),
            pltpu.VMEM((2, 1, 96), I32),
            pltpu.VMEM((2, NX, NY, MAIN, PACKED), BF16),
            pltpu.VMEM((NAUX, NAUX), BF16),
            pltpu.VMEM((CHUNKS, 64, 192), BF16),
            pltpu.VMEM((CHUNKS, 8, LANES), F32),
            pltpu.VMEM((CHUNKS, 2 * NZ, 8, LANES), F32),
            pltpu.VMEM((NX * NY, 1, LANES), F32),
            pltpu.VMEM((NX * NY, 1, LANES), F32),
            dma((3 + CHUNKS,)),
            dma((CHUNKS, NZ)), dma((CHUNKS, NZ)),
            dma((NZ,)), dma((NZ,)),
            dma, dma,
            dma((NY,)), dma((NY,)),
            dma((NX,)), dma((NX,)),
            dma((NX,)), dma((NX,)),
            dma((CHUNKS, 2, NZ)), dma((CHUNKS,)),
            dma((NX * NY,)), dma,
        ],
        compiler_params=pltpu.CompilerParams(collective_id=0, has_side_effects=True),
    )(integrals, tile_mask, metric, owners.reshape(1, -1))


def solution(mesh):
    return jax.shard_map(
        body,
        mesh=mesh,
        in_specs=(P("aux", "pair"), P("aux", "pair"), P("pair", None), P("pair")),
        out_specs=P(("aux", "pair"), None),
        check_vma=False,
    )
```

```python
import functools

import jax
import jax.numpy as jnp
from jax import lax
from jax.experimental import pallas as pl
from jax.experimental.pallas import tpu as pltpu
from jax.sharding import PartitionSpec as P

MESH = pl.DeviceIdType.MESH
F32, BF16, I32 = jnp.float32, jnp.bfloat16, jnp.int32
NZ, NX, NY = 12, 4, 8
AUXD, WIDTH, NAUX = 96, 512, 1152
CHUNKS = 2
CW = WIDTH // CHUNKS
LANES = 128
SHARD = 18
MAIN = 16
PACKED = NAUX + 2 * LANES
QB = 576
ORDER = (6, 5, 7, 4, 8, 3, 9, 2, 10, 1, 11)
AROUND = sorted(
    [(i, j) for i in range(NX) for j in range(NY) if i or j], key=lambda k: -min(k[0], NX - k[0]) - min(k[1], NY - k[1])
)


def iota(shape, axis):
    return lax.broadcasted_iota(I32, shape, axis)


def kernel(
    x_hbm, mask_hbm, met_hbm, own_hbm, out_ref,
    got, masks, keep, met, own, slots, dense, hits, terms, heard, part, rows_in,
    in_sem, z_send, z_recv, m_send, m_recv, o_send, o_recv, y_send, y_recv, x_send, x_recv, c_send, c_recv,
    t_send, t_recv, p_send, p_recv,
):
    z = lax.axis_index("aux")
    pair = lax.axis_index("pair")
    c = pair & 1
    y = (pair >> 1) & (NY - 1)
    x = pair >> 4
    place = pair >> 1

    ahead = [z] + [jnp.where(z + k >= NZ, z + k - NZ, z + k) for k in range(1, NZ)]

    def at_z(k):
        return ahead[k]

    def at_y(k):
        return (y + k) & (NY - 1)

    def dev_z(k):
        return {"aux": at_z(k)}

    def dev_zc(k, flip):
        return {"aux": at_z(k), "pair": pair ^ 1 if flip else pair}

    def dev_y(k):
        return {"pair": (x * NY + at_y(k)) * 2 + c}

    def place_at(k):
        return ((x + k[0]) & (NX - 1)) * NY + ((y + k[1]) & (NY - 1))

    def dev_xy(k):
        return {"pair": place_at(k) * 2 + c}

    def dev_x(k):
        return {"pair": (((x + k) & (NX - 1)) * NY + y) * 2 + c}

    dev_c = {"pair": pair ^ 1}

    def remote(s, d, ss, rs, dev):
        return pltpu.make_async_remote_copy(src_ref=s, dst_ref=d, send_sem=ss, recv_sem=rs, device_id=dev, device_id_type=MESH)

    def columns(block, j):
        return x_hbm.at[:, pl.ds(pl.multiple_of(block * WIDTH + j * CW, LANES), CW)]

    met_in = pltpu.make_async_copy(met_hbm, met, in_sem.at[0])
    met_in.start()
    barrier = pltpu.get_barrier_semaphore()
    peers = [dev_zc(k, False) for k in ORDER] + [dev_xy(k) for k in AROUND] + [dev_zc(k, True) for k in ORDER + (0,)]
    for peer in peers:
        pl.semaphore_signal(barrier, inc=1, device_id=peer, device_id_type=MESH)
    locals_in = [
        pltpu.make_async_copy(mask_hbm, masks.at[z], in_sem.at[1]),
        pltpu.make_async_copy(own_hbm, own.at[c], in_sem.at[2]),
    ] + [pltpu.make_async_copy(columns(z, j), got.at[j, z], in_sem.at[3 + j]) for j in range(CHUNKS)]
    for copy in locals_in:
        copy.start()
    met_in.wait()
    rows = met[...].astype(F32)
    tail = rows[MAIN:SHARD]
    rest = jnp.concatenate([tail[:, i * LANES : (i + 1) * LANES] for i in range(8)], axis=0)
    last = jnp.concatenate([tail[:, 8 * LANES :], jnp.zeros((MAIN - 2, LANES), F32)], axis=0)
    slots[c, x, y] = jnp.concatenate([rows[:MAIN], rest, last], axis=1).astype(BF16)
    pl.semaphore_wait(barrier, len(peers))

    z_copies = [
        [remote(columns(at_z(k), j), got.at[j, z], z_send.at[j, k], z_recv.at[j, k], dev_z(k)) for k in ORDER]
        for j in range(CHUNKS)
    ]
    m_copies = [remote(mask_hbm, masks.at[z], m_send.at[k], m_recv.at[k], dev_z(k)) for k in ORDER]
    y_copies = [remote(slots.at[c, x, y], slots.at[c, x, y], y_send.at[k], y_recv.at[k], dev_y(k)) for k in range(1, NY)]
    for copy in y_copies:
        copy.start()
    o_copy = remote(own_hbm, own.at[c], o_send, o_recv, dev_c)
    o_copy.start()
    for copy in m_copies:
        copy.start()
    for group, ks in ((0, ORDER[:7]), (1, ORDER[:7]), (0, ORDER[7:]), (1, ORDER[7:])):
        for k in ks:
            z_copies[group][ORDER.index(k)].start()

    for copy in locals_in:
        copy.wait()
    for k in ORDER:
        there = at_z((NZ - k) % NZ)
        remote(mask_hbm, masks.at[there], m_send.at[k], m_recv.at[k], dev_z(k)).wait_recv()
    spread = jnp.where(iota((96, WIDTH), 0) == z * 8 + (iota((96, WIDTH), 1) >> 6), 1.0, 0.0).astype(BF16)
    entries = jnp.concatenate([masks[a] for a in range(NZ)] + [jnp.zeros((4, 96), I32)], axis=0).astype(F32).astype(BF16)
    keep[...] = jnp.dot(entries, spread, preferred_element_type=F32)

    remote(own_hbm, own.at[1 - c], o_send, o_recv, dev_c).wait_recv()
    target = z * 64 + iota((32, 96), 0) * 2 + c
    q = iota((96, 192), 1)
    t = iota((96, 192), 0)
    for j in range(CHUNKS):
        for par in range(2):
            picked = jnp.zeros((32, 192), F32)
            for core in range(2):
                qq = q - 96 * core
                wanted = (qq >> 3) * 8 + 2 * (j * (CW // LANES) + (qq & 7)) + par
                perm = jnp.where((t == wanted) & ((qq & 7) < CW // LANES) & (qq >= 0) & (qq < 96), 1.0, 0.0).astype(BF16)
                hit = jnp.where(own[core] == target, 1.0, 0.0).astype(BF16)
                picked = picked + jnp.dot(hit, perm, preferred_element_type=F32)
            hits[j, pl.ds(par * 32, 32), :] = picked.astype(BF16)

    def from_y(k):
        there = ((y - k) & (NY - 1))
        return remote(slots.at[c, x, there], slots.at[c, x, there], y_send.at[k], y_recv.at[k], dev_y(k))

    for k in range(1, NY):
        from_y(k).wait_recv()
    x_copies = [remote(slots.at[c, x], slots.at[c, x], x_send.at[k], x_recv.at[k], dev_x(k)) for k in (2, 1, 3)]
    for copy in x_copies:
        copy.start()

    def between(k, core):
        there = ((x - k) & (NX - 1))
        return remote(slots.at[core, there], slots.at[core, there], c_send.at[k], c_recv.at[k], dev_c)

    row = iota((288, 256), 0)
    col = iota((288, 256), 1)
    yy = jnp.zeros_like(row)
    for step in range(1, NY):
        yy = yy + (row >= 36 * step).astype(I32)
    row = row - 36 * yy
    cc = (row >= SHARD).astype(I32)
    row = row - SHARD * cc
    first_rows = jnp.where((row < MAIN) & (col == cc * 128 + yy * MAIN + row), 1.0, 0.0).astype(BF16)
    last_rows = jnp.where((row >= MAIN) & (col == cc * 16 + yy * 2 + row - MAIN), 1.0, 0.0).astype(BF16)[:, :32]
    row = iota((256, 256), 0)
    col = iota((256, 256), 1)
    slot = (row & 31) >> 1
    regroup = jnp.where(col == slot * MAIN + 2 * (row >> 5) + (row & 1), 1.0, 0.0).astype(BF16)

    def spread_rows(k):
        there = ((x - k) & (NX - 1))
        rest = [slots[:, there, :, :, pl.ds(NAUX + i * LANES, LANES)].reshape(256, LANES) for i in range(2)]
        pieces = jnp.dot(regroup, rest[0], preferred_element_type=F32).astype(BF16)
        piece = jnp.dot(regroup[:32], rest[1], preferred_element_type=F32).astype(BF16)
        ends = jnp.concatenate([pieces[32 * i : 32 * (i + 1)] for i in range(8)] + [piece], axis=1)
        for i in range(3):
            cols = pl.ds(i * 384, 384)
            main = slots[:, there, :, :, cols].reshape(256, 384)
            both = jnp.dot(first_rows, main, preferred_element_type=F32)
            both = both + jnp.dot(last_rows, ends[:, i * 384 : (i + 1) * 384], preferred_element_type=F32)
            dense[pl.ds(pl.multiple_of(there * 288, 32), 288), cols] = both.astype(BF16)

    c_copies = [between(k, c) for k in range(NX)]
    c_copies[0].start()
    for k, before in ((1, 0), (3, 1), (2, 3)):
        there = ((x - k) & (NX - 1))
        remote(slots.at[c, there], slots.at[c, there], x_send.at[k], x_recv.at[k], dev_x(k)).wait_recv()
        c_copies[k].start()
        between(before, 1 - c).wait_recv()
        spread_rows(before)
    between(2, 1 - c).wait_recv()
    spread_rows(2)

    def chunk(j):
        for k in (0,) + ORDER:
            there = at_z((NZ - k) % NZ)
            if k:
                remote(columns(there, j), got.at[j, there], z_send.at[j, k], z_recv.at[j, k], dev_z(k)).wait_recv()
            got[j, there] = got[j, there] * keep[pl.ds(there, 1), pl.ds(j * CW, CW)].astype(BF16)
        block = got[j].reshape(NAUX, CW)
        acc = jnp.zeros((1, CW), F32)
        for i in range(NAUX // QB):
            image = jnp.dot(dense[pl.ds(i * QB, QB), :], block, preferred_element_type=F32)
            acc = acc + jnp.sum(block[i * QB : (i + 1) * QB].astype(F32) * image, axis=0, keepdims=True)
        pieces = [acc[:, i * LANES : (i + 1) * LANES] for i in range(CW // LANES)]
        terms[j] = jnp.concatenate(pieces + [jnp.zeros((8 - len(pieces), LANES), F32)], axis=0)
        copies = [
            remote(terms.at[j], heard.at[j, c * NZ + z], t_send.at[j, int(flip), k], t_recv.at[j], dev_zc(k, flip))
            for k in ORDER + (0,) for flip in (False, True) if k or flip
        ]
        for copy in copies:
            copy.start()
        heard[j, c * NZ + z] = terms[j]
        return copies

    def owned(j):
        others = heard.at[j, pl.ds(0, 2 * NZ - 1)]
        pltpu.make_async_copy(others, others, t_recv.at[j]).wait()
        value = heard[j].reshape(192, LANES)
        first = value.astype(BF16)
        value = value - first.astype(F32)
        second = value.astype(BF16)
        third = (value - second.astype(F32)).astype(BF16)
        sums = [jnp.dot(hits[j], v, preferred_element_type=F32) for v in (third, second, first)]
        both = sums[0] + sums[1] + sums[2]
        return jnp.where(iota((32, LANES), 1) < 64, both[:32], both[32:])

    t_copies = [chunk(0)]
    total = None
    for j in range(1, CHUNKS):
        t_copies.append(chunk(j))
        mine = owned(j - 1)
        total = mine if total is None else total + mine
    for group in [y_copies, x_copies, c_copies, [o_copy], m_copies] + z_copies + t_copies:
        for copy in group:
            copy.wait_send()
    mine = owned(CHUNKS - 1)
    total = mine if total is None else total + mine

    for i in range(NX * NY):
        part[i] = total[i : i + 1]
    p_copies = [
        remote(part.at[place_at(k)], rows_in.at[place], p_send.at[i], p_recv, dev_xy(k)) for i, k in enumerate(AROUND)
    ]
    for copy in p_copies:
        copy.start()
    rows_in[place] = part[place]
    for copy in p_copies:
        copy.wait_send()
    others = rows_in.at[pl.ds(0, NX * NY - 1)]
    pltpu.make_async_copy(others, others, p_recv).wait()
    both = jnp.sum(rows_in[...], axis=0)
    out_ref[...] = both[:, :64] + both[:, 64:]


def body(integrals, tile_mask, metric, owners):
    any_spec = pl.BlockSpec(memory_space=pl.ANY)
    dma = pltpu.SemaphoreType.DMA
    return pl.pallas_call(
        kernel,
        out_shape=jax.ShapeDtypeStruct((1, 64), F32),
        in_specs=[any_spec] * 4,
        out_specs=pl.BlockSpec(memory_space=pltpu.VMEM),
        scratch_shapes=[
            pltpu.VMEM((CHUNKS, NZ, AUXD, CW), BF16),
            pltpu.VMEM((NZ, 1, 96), I32),
            pltpu.VMEM((16, WIDTH), F32),
            pltpu.VMEM((SHARD, NAUX), BF16),
            pltpu.VMEM((2, 1, 96), I32),
            pltpu.VMEM((2, NX, NY, MAIN, PACKED), BF16),
            pltpu.VMEM((NAUX, NAUX), BF16),
            pltpu.VMEM((CHUNKS, 64, 192), BF16),
            pltpu.VMEM((CHUNKS, 8, LANES), F32),
            pltpu.VMEM((CHUNKS, 2 * NZ, 8, LANES), F32),
            pltpu.VMEM((NX * NY, 1, LANES), F32),
            pltpu.VMEM((NX * NY, 1, LANES), F32),
            dma((3 + CHUNKS,)),
            dma((CHUNKS, NZ)), dma((CHUNKS, NZ)),
            dma((NZ,)), dma((NZ,)),
            dma, dma,
            dma((NY,)), dma((NY,)),
            dma((NX,)), dma((NX,)),
            dma((NX,)), dma((NX,)),
            dma((CHUNKS, 2, NZ)), dma((CHUNKS,)),
            dma((NX * NY,)), dma,
        ],
        compiler_params=pltpu.CompilerParams(collective_id=0, has_side_effects=True),
    )(integrals, tile_mask, metric, owners.reshape(1, -1))


def solution(mesh):
    return jax.shard_map(
        body,
        mesh=mesh,
        in_specs=(P("aux", "pair"), P("aux", "pair"), P("pair", None), P("pair")),
        out_specs=P(("aux", "pair"), None),
        check_vma=False,
    )
```

```python
import functools

import jax
import jax.numpy as jnp
from jax import lax
from jax.experimental import pallas as pl
from jax.experimental.pallas import tpu as pltpu
from jax.sharding import PartitionSpec as P

MESH = pl.DeviceIdType.MESH
F32, BF16, I32 = jnp.float32, jnp.bfloat16, jnp.int32
NZ, NX, NY = 12, 4, 8
AUXD, WIDTH, NAUX = 96, 512, 1152
CHUNKS = 2
CW = WIDTH // CHUNKS
LANES = 128
SHARD = 18
MAIN = 16
PACKED = NAUX + 2 * LANES
QB = 576
ORDER = (6, 5, 7, 4, 8, 3, 9, 2, 10, 1, 11)
AROUND = sorted(
    [(i, j) for i in range(NX) for j in range(NY) if i or j], key=lambda k: -min(k[0], NX - k[0]) - min(k[1], NY - k[1])
)


def iota(shape, axis):
    return lax.broadcasted_iota(I32, shape, axis)


def kernel(
    x_hbm, mask_hbm, met_hbm, own_hbm, out_ref,
    got, masks, keep, met, own, slots, dense, hits, terms, heard, part, rows_in,
    in_sem, z_send, z_recv, m_send, m_recv, o_send, o_recv, y_send, y_recv, x_send, x_recv, c_send, c_recv,
    t_send, t_recv, p_send, p_recv,
):
    z = lax.axis_index("aux")
    pair = lax.axis_index("pair")
    c = pair & 1
    y = (pair >> 1) & (NY - 1)
    x = pair >> 4
    place = pair >> 1

    ahead = [z] + [jnp.where(z + k >= NZ, z + k - NZ, z + k) for k in range(1, NZ)]

    def at_z(k):
        return ahead[k]

    def at_y(k):
        return (y + k) & (NY - 1)

    def dev_z(k):
        return {"aux": at_z(k)}

    def dev_zc(k, flip):
        return {"aux": at_z(k), "pair": pair ^ 1 if flip else pair}

    def dev_y(k):
        return {"pair": (x * NY + at_y(k)) * 2 + c}

    def place_at(k):
        return ((x + k[0]) & (NX - 1)) * NY + ((y + k[1]) & (NY - 1))

    def dev_xy(k):
        return {"pair": place_at(k) * 2 + c}

    def dev_x(k):
        return {"pair": (((x + k) & (NX - 1)) * NY + y) * 2 + c}

    dev_c = {"pair": pair ^ 1}

    def remote(s, d, ss, rs, dev):
        return pltpu.make_async_remote_copy(src_ref=s, dst_ref=d, send_sem=ss, recv_sem=rs, device_id=dev, device_id_type=MESH)

    def columns(block, j):
        return x_hbm.at[:, pl.ds(pl.multiple_of(block * WIDTH + j * CW, LANES), CW)]

    met_in = pltpu.make_async_copy(met_hbm, met, in_sem.at[0])
    met_in.start()
    barrier = pltpu.get_barrier_semaphore()
    peers = [dev_zc(k, False) for k in ORDER] + [dev_xy(k) for k in AROUND if 0 in k] + [dev_zc(0, True)]
    for peer in peers:
        pl.semaphore_signal(barrier, inc=1, device_id=peer, device_id_type=MESH)
    locals_in = [
        pltpu.make_async_copy(mask_hbm, masks.at[z], in_sem.at[1]),
        pltpu.make_async_copy(own_hbm, own.at[c], in_sem.at[2]),
    ] + [pltpu.make_async_copy(columns(z, j), got.at[j, z], in_sem.at[3 + j]) for j in range(CHUNKS)]
    for copy in locals_in:
        copy.start()
    met_in.wait()
    rows = met[...].astype(F32)
    tail = rows[MAIN:SHARD]
    rest = jnp.concatenate([tail[:, i * LANES : (i + 1) * LANES] for i in range(8)], axis=0)
    last = jnp.concatenate([tail[:, 8 * LANES :], jnp.zeros((MAIN - 2, LANES), F32)], axis=0)
    slots[c, x, y] = jnp.concatenate([rows[:MAIN], rest, last], axis=1).astype(BF16)
    pl.semaphore_wait(barrier, len(peers))

    z_copies = [
        [remote(columns(at_z(k), j), got.at[j, z], z_send.at[j, k], z_recv.at[j, k], dev_z(k)) for k in ORDER]
        for j in range(CHUNKS)
    ]
    m_copies = [remote(mask_hbm, masks.at[z], m_send.at[k], m_recv.at[k], dev_z(k)) for k in ORDER]
    y_copies = [remote(slots.at[c, x, y], slots.at[c, x, y], y_send.at[k], y_recv.at[k], dev_y(k)) for k in range(1, NY)]
    for copy in y_copies:
        copy.start()
    o_copy = remote(own_hbm, own.at[c], o_send, o_recv, dev_c)
    o_copy.start()
    for copy in m_copies:
        copy.start()
    for group, ks in ((0, ORDER[:7]), (1, ORDER[:7]), (0, ORDER[7:]), (1, ORDER[7:])):
        for k in ks:
            z_copies[group][ORDER.index(k)].start()

    for copy in locals_in:
        copy.wait()
    for k in ORDER:
        there = at_z((NZ - k) % NZ)
        remote(mask_hbm, masks.at[there], m_send.at[k], m_recv.at[k], dev_z(k)).wait_recv()
    spread = jnp.where(iota((96, WIDTH), 0) == z * 8 + (iota((96, WIDTH), 1) >> 6), 1.0, 0.0).astype(BF16)
    entries = jnp.concatenate([masks[a] for a in range(NZ)] + [jnp.zeros((4, 96), I32)], axis=0).astype(F32).astype(BF16)
    keep[...] = jnp.dot(entries, spread, preferred_element_type=F32)

    remote(own_hbm, own.at[1 - c], o_send, o_recv, dev_c).wait_recv()
    target = z * 64 + iota((32, 96), 0) * 2 + c
    q = iota((96, 192), 1)
    t = iota((96, 192), 0)
    for j in range(CHUNKS):
        for par in range(2):
            picked = jnp.zeros((32, 192), F32)
            for core in range(2):
                qq = q - 96 * core
                wanted = (qq >> 3) * 8 + 2 * (j * (CW // LANES) + (qq & 7)) + par
                perm = jnp.where((t == wanted) & ((qq & 7) < CW // LANES) & (qq >= 0) & (qq < 96), 1.0, 0.0).astype(BF16)
                hit = jnp.where(own[core] == target, 1.0, 0.0).astype(BF16)
                picked = picked + jnp.dot(hit, perm, preferred_element_type=F32)
            hits[j, pl.ds(par * 32, 32), :] = picked.astype(BF16)

    def from_y(k):
        there = ((y - k) & (NY - 1))
        return remote(slots.at[c, x, there], slots.at[c, x, there], y_send.at[k], y_recv.at[k], dev_y(k))

    for k in range(1, NY):
        from_y(k).wait_recv()
    x_copies = [remote(slots.at[c, x], slots.at[c, x], x_send.at[k], x_recv.at[k], dev_x(k)) for k in (2, 1, 3)]
    for copy in x_copies:
        copy.start()

    def between(k, core):
        there = ((x - k) & (NX - 1))
        return remote(slots.at[core, there], slots.at[core, there], c_send.at[k], c_recv.at[k], dev_c)

    row = iota((288, 256), 0)
    col = iota((288, 256), 1)
    yy = jnp.zeros_like(row)
    for step in range(1, NY):
        yy = yy + (row >= 36 * step).astype(I32)
    row = row - 36 * yy
    cc = (row >= SHARD).astype(I32)
    row = row - SHARD * cc
    first_rows = jnp.where((row < MAIN) & (col == cc * 128 + yy * MAIN + row), 1.0, 0.0).astype(BF16)
    last_rows = jnp.where((row >= MAIN) & (col == cc * 16 + yy * 2 + row - MAIN), 1.0, 0.0).astype(BF16)[:, :32]
    row = iota((256, 256), 0)
    col = iota((256, 256), 1)
    slot = (row & 31) >> 1
    regroup = jnp.where(col == slot * MAIN + 2 * (row >> 5) + (row & 1), 1.0, 0.0).astype(BF16)

    def spread_rows(k):
        there = ((x - k) & (NX - 1))
        rest = [slots[:, there, :, :, pl.ds(NAUX + i * LANES, LANES)].reshape(256, LANES) for i in range(2)]
        pieces = jnp.dot(regroup, rest[0], preferred_element_type=F32).astype(BF16)
        piece = jnp.dot(regroup[:32], rest[1], preferred_element_type=F32).astype(BF16)
        ends = jnp.concatenate([pieces[32 * i : 32 * (i + 1)] for i in range(8)] + [piece], axis=1)
        for i in range(3):
            cols = pl.ds(i * 384, 384)
            main = slots[:, there, :, :, cols].reshape(256, 384)
            both = jnp.dot(first_rows, main, preferred_element_type=F32)
            both = both + jnp.dot(last_rows, ends[:, i * 384 : (i + 1) * 384], preferred_element_type=F32)
            dense[pl.ds(pl.multiple_of(there * 288, 32), 288), cols] = both.astype(BF16)

    c_copies = [between(k, c) for k in range(NX)]
    c_copies[0].start()
    for k, before in ((1, 0), (3, 1), (2, 3)):
        there = ((x - k) & (NX - 1))
        remote(slots.at[c, there], slots.at[c, there], x_send.at[k], x_recv.at[k], dev_x(k)).wait_recv()
        c_copies[k].start()
        between(before, 1 - c).wait_recv()
        spread_rows(before)
    between(2, 1 - c).wait_recv()
    spread_rows(2)

    def chunk(j):
        for k in (0,) + ORDER:
            there = at_z((NZ - k) % NZ)
            if k:
                remote(columns(there, j), got.at[j, there], z_send.at[j, k], z_recv.at[j, k], dev_z(k)).wait_recv()
            got[j, there] = got[j, there] * keep[pl.ds(there, 1), pl.ds(j * CW, CW)].astype(BF16)
        block = got[j].reshape(NAUX, CW)
        acc = jnp.zeros((1, CW), F32)
        for i in range(NAUX // QB):
            image = jnp.dot(dense[pl.ds(i * QB, QB), :], block, preferred_element_type=F32)
            acc = acc + jnp.sum(block[i * QB : (i + 1) * QB].astype(F32) * image, axis=0, keepdims=True)
        pieces = [acc[:, i * LANES : (i + 1) * LANES] for i in range(CW // LANES)]
        terms[j] = jnp.concatenate(pieces + [jnp.zeros((8 - len(pieces), LANES), F32)], axis=0)
        copies = [
            remote(terms.at[j], heard.at[j, c * NZ + z], t_send.at[j, int(flip), k], t_recv.at[j], dev_zc(k, flip))
            for k in ORDER + (0,) for flip in (False, True) if k or flip
        ]
        for copy in copies:
            copy.start()
        heard[j, c * NZ + z] = terms[j]
        return copies

    def owned(j):
        others = heard.at[j, pl.ds(0, 2 * NZ - 1)]
        pltpu.make_async_copy(others, others, t_recv.at[j]).wait()
        value = heard[j].reshape(192, LANES)
        first = value.astype(BF16)
        value = value - first.astype(F32)
        second = value.astype(BF16)
        third = (value - second.astype(F32)).astype(BF16)
        sums = [jnp.dot(hits[j], v, preferred_element_type=F32) for v in (third, second, first)]
        both = sums[0] + sums[1] + sums[2]
        return jnp.where(iota((32, LANES), 1) < 64, both[:32], both[32:])

    t_copies = [chunk(0)]
    total = None
    for j in range(1, CHUNKS):
        t_copies.append(chunk(j))
        mine = owned(j - 1)
        total = mine if total is None else total + mine
    for group in [y_copies, x_copies, c_copies, [o_copy], m_copies] + z_copies + t_copies:
        for copy in group:
            copy.wait_send()
    mine = owned(CHUNKS - 1)
    total = mine if total is None else total + mine

    for i in range(NX * NY):
        part[i] = total[i : i + 1]
    p_copies = [
        remote(part.at[place_at(k)], rows_in.at[place], p_send.at[i], p_recv, dev_xy(k)) for i, k in enumerate(AROUND)
    ]
    for copy in p_copies:
        copy.start()
    rows_in[place] = part[place]
    for copy in p_copies:
        copy.wait_send()
    others = rows_in.at[pl.ds(0, NX * NY - 1)]
    pltpu.make_async_copy(others, others, p_recv).wait()
    both = jnp.sum(rows_in[...], axis=0)
    out_ref[...] = both[:, :64] + both[:, 64:]


def body(integrals, tile_mask, metric, owners):
    any_spec = pl.BlockSpec(memory_space=pl.ANY)
    dma = pltpu.SemaphoreType.DMA
    return pl.pallas_call(
        kernel,
        out_shape=jax.ShapeDtypeStruct((1, 64), F32),
        in_specs=[any_spec] * 4,
        out_specs=pl.BlockSpec(memory_space=pltpu.VMEM),
        scratch_shapes=[
            pltpu.VMEM((CHUNKS, NZ, AUXD, CW), BF16),
            pltpu.VMEM((NZ, 1, 96), I32),
            pltpu.VMEM((16, WIDTH), F32),
            pltpu.VMEM((SHARD, NAUX), BF16),
            pltpu.VMEM((2, 1, 96), I32),
            pltpu.VMEM((2, NX, NY, MAIN, PACKED), BF16),
            pltpu.VMEM((NAUX, NAUX), BF16),
            pltpu.VMEM((CHUNKS, 64, 192), BF16),
            pltpu.VMEM((CHUNKS, 8, LANES), F32),
            pltpu.VMEM((CHUNKS, 2 * NZ, 8, LANES), F32),
            pltpu.VMEM((NX * NY, 1, LANES), F32),
            pltpu.VMEM((NX * NY, 1, LANES), F32),
            dma((3 + CHUNKS,)),
            dma((CHUNKS, NZ)), dma((CHUNKS, NZ)),
            dma((NZ,)), dma((NZ,)),
            dma, dma,
            dma((NY,)), dma((NY,)),
            dma((NX,)), dma((NX,)),
            dma((NX,)), dma((NX,)),
            dma((CHUNKS, 2, NZ)), dma((CHUNKS,)),
            dma((NX * NY,)), dma,
        ],
        compiler_params=pltpu.CompilerParams(collective_id=0, has_side_effects=True),
    )(integrals, tile_mask, metric, owners.reshape(1, -1))


def solution(mesh):
    return jax.shard_map(
        body,
        mesh=mesh,
        in_specs=(P("aux", "pair"), P("aux", "pair"), P("pair", None), P("pair")),
        out_specs=P(("aux", "pair"), None),
        check_vma=False,
    )
```

```python
import functools

import jax
import jax.numpy as jnp
from jax import lax
from jax.experimental import pallas as pl
from jax.experimental.pallas import tpu as pltpu
from jax.sharding import PartitionSpec as P

MESH = pl.DeviceIdType.MESH
F32, BF16, I32 = jnp.float32, jnp.bfloat16, jnp.int32
NZ, NX, NY = 12, 4, 8
AUXD, WIDTH, NAUX = 96, 512, 1152
CHUNKS = 2
CW = WIDTH // CHUNKS
LANES = 128
SHARD = 18
MAIN = 16
PACKED = NAUX + 2 * LANES
QB = 576
ORDER = (6, 5, 7, 4, 8, 3, 9, 2, 10, 1, 11)
AROUND = sorted(
    [(i, j) for i in range(NX) for j in range(NY) if i or j], key=lambda k: -min(k[0], NX - k[0]) - min(k[1], NY - k[1])
)


def iota(shape, axis):
    return lax.broadcasted_iota(I32, shape, axis)


def kernel(
    x_hbm, mask_hbm, met_hbm, own_hbm, out_ref,
    got, masks, keep, met, own, slots, dense, hits, terms, heard, part, rows_in,
    in_sem, z_send, z_recv, m_send, m_recv, o_send, o_recv, y_send, y_recv, x_send, x_recv, c_send, c_recv,
    t_send, t_recv, p_send, p_recv,
):
    z = lax.axis_index("aux")
    pair = lax.axis_index("pair")
    c = pair & 1
    y = (pair >> 1) & (NY - 1)
    x = pair >> 4
    place = pair >> 1

    ahead = [z] + [jnp.where(z + k >= NZ, z + k - NZ, z + k) for k in range(1, NZ)]

    def at_z(k):
        return ahead[k]

    def at_y(k):
        return (y + k) & (NY - 1)

    def dev_z(k):
        return {"aux": at_z(k)}

    def dev_zc(k, flip):
        return {"aux": at_z(k), "pair": pair ^ 1 if flip else pair}

    def dev_y(k):
        return {"pair": (x * NY + at_y(k)) * 2 + c}

    def place_at(k):
        return ((x + k[0]) & (NX - 1)) * NY + ((y + k[1]) & (NY - 1))

    def dev_xy(k):
        return {"pair": place_at(k) * 2 + c}

    def dev_x(k):
        return {"pair": (((x + k) & (NX - 1)) * NY + y) * 2 + c}

    dev_c = {"pair": pair ^ 1}

    def remote(s, d, ss, rs, dev):
        return pltpu.make_async_remote_copy(src_ref=s, dst_ref=d, send_sem=ss, recv_sem=rs, device_id=dev, device_id_type=MESH)

    def columns(block, j):
        return x_hbm.at[:, pl.ds(pl.multiple_of(block * WIDTH + j * CW, LANES), CW)]

    met_in = pltpu.make_async_copy(met_hbm, met, in_sem.at[0])
    met_in.start()
    barrier = pltpu.get_barrier_semaphore()
    peers = [dev_zc(k, False) for k in ORDER] + [dev_xy(k) for k in AROUND if 0 in k] + [dev_zc(0, True)]
    for peer in peers:
        pl.semaphore_signal(barrier, inc=1, device_id=peer, device_id_type=MESH)
    locals_in = [
        pltpu.make_async_copy(mask_hbm, masks.at[z], in_sem.at[1]),
        pltpu.make_async_copy(own_hbm, own.at[c], in_sem.at[2]),
    ] + [pltpu.make_async_copy(columns(z, j), got.at[j, z], in_sem.at[3 + j]) for j in range(CHUNKS)]
    for copy in locals_in:
        copy.start()
    pl.semaphore_wait(barrier, len(peers))

    z_copies = [
        [remote(columns(at_z(k), j), got.at[j, z], z_send.at[j, k], z_recv.at[j, k], dev_z(k)) for k in ORDER]
        for j in range(CHUNKS)
    ]
    m_copies = [remote(mask_hbm, masks.at[z], m_send.at[k], m_recv.at[k], dev_z(k)) for k in ORDER]
    for copy in m_copies:
        copy.start()
    for copy in z_copies[0][:2]:
        copy.start()
    met_in.wait()
    rows = met[...].astype(F32)
    tail = rows[MAIN:SHARD]
    rest = jnp.concatenate([tail[:, i * LANES : (i + 1) * LANES] for i in range(8)], axis=0)
    last = jnp.concatenate([tail[:, 8 * LANES :], jnp.zeros((MAIN - 2, LANES), F32)], axis=0)
    slots[c, x, y] = jnp.concatenate([rows[:MAIN], rest, last], axis=1).astype(BF16)
    y_copies = [remote(slots.at[c, x, y], slots.at[c, x, y], y_send.at[k], y_recv.at[k], dev_y(k)) for k in range(1, NY)]
    for copy in y_copies:
        copy.start()
    o_copy = remote(own_hbm, own.at[c], o_send, o_recv, dev_c)
    o_copy.start()
    for group, ks in ((0, ORDER[2:7]), (1, ORDER[:7]), (0, ORDER[7:]), (1, ORDER[7:])):
        for k in ks:
            z_copies[group][ORDER.index(k)].start()

    for copy in locals_in:
        copy.wait()
    for k in ORDER:
        there = at_z((NZ - k) % NZ)
        remote(mask_hbm, masks.at[there], m_send.at[k], m_recv.at[k], dev_z(k)).wait_recv()
    spread = jnp.where(iota((96, WIDTH), 0) == z * 8 + (iota((96, WIDTH), 1) >> 6), 1.0, 0.0).astype(BF16)
    entries = jnp.concatenate([masks[a] for a in range(NZ)] + [jnp.zeros((4, 96), I32)], axis=0).astype(F32).astype(BF16)
    keep[...] = jnp.dot(entries, spread, preferred_element_type=F32)

    remote(own_hbm, own.at[1 - c], o_send, o_recv, dev_c).wait_recv()
    target = z * 64 + iota((32, 96), 0) * 2 + c
    q = iota((96, 192), 1)
    t = iota((96, 192), 0)
    for j in range(CHUNKS):
        for par in range(2):
            picked = jnp.zeros((32, 192), F32)
            for core in range(2):
                qq = q - 96 * core
                wanted = (qq >> 3) * 8 + 2 * (j * (CW // LANES) + (qq & 7)) + par
                perm = jnp.where((t == wanted) & ((qq & 7) < CW // LANES) & (qq >= 0) & (qq < 96), 1.0, 0.0).astype(BF16)
                hit = jnp.where(own[core] == target, 1.0, 0.0).astype(BF16)
                picked = picked + jnp.dot(hit, perm, preferred_element_type=F32)
            hits[j, pl.ds(par * 32, 32), :] = picked.astype(BF16)

    def from_y(k):
        there = ((y - k) & (NY - 1))
        return remote(slots.at[c, x, there], slots.at[c, x, there], y_send.at[k], y_recv.at[k], dev_y(k))

    for k in range(1, NY):
        from_y(k).wait_recv()
    x_copies = [remote(slots.at[c, x], slots.at[c, x], x_send.at[k], x_recv.at[k], dev_x(k)) for k in (2, 1, 3)]
    for copy in x_copies:
        copy.start()

    def between(k, core):
        there = ((x - k) & (NX - 1))
        return remote(slots.at[core, there], slots.at[core, there], c_send.at[k], c_recv.at[k], dev_c)

    row = iota((288, 256), 0)
    col = iota((288, 256), 1)
    yy = jnp.zeros_like(row)
    for step in range(1, NY):
        yy = yy + (row >= 36 * step).astype(I32)
    row = row - 36 * yy
    cc = (row >= SHARD).astype(I32)
    row = row - SHARD * cc
    first_rows = jnp.where((row < MAIN) & (col == cc * 128 + yy * MAIN + row), 1.0, 0.0).astype(BF16)
    last_rows = jnp.where((row >= MAIN) & (col == cc * 16 + yy * 2 + row - MAIN), 1.0, 0.0).astype(BF16)[:, :32]
    row = iota((256, 256), 0)
    col = iota((256, 256), 1)
    slot = (row & 31) >> 1
    regroup = jnp.where(col == slot * MAIN + 2 * (row >> 5) + (row & 1), 1.0, 0.0).astype(BF16)

    def spread_rows(k):
        there = ((x - k) & (NX - 1))
        rest = [slots[:, there, :, :, pl.ds(NAUX + i * LANES, LANES)].reshape(256, LANES) for i in range(2)]
        pieces = jnp.dot(regroup, rest[0], preferred_element_type=F32).astype(BF16)
        piece = jnp.dot(regroup[:32], rest[1], preferred_element_type=F32).astype(BF16)
        ends = jnp.concatenate([pieces[32 * i : 32 * (i + 1)] for i in range(8)] + [piece], axis=1)
        for i in range(3):
            cols = pl.ds(i * 384, 384)
            main = slots[:, there, :, :, cols].reshape(256, 384)
            both = jnp.dot(first_rows, main, preferred_element_type=F32)
            both = both + jnp.dot(last_rows, ends[:, i * 384 : (i + 1) * 384], preferred_element_type=F32)
            dense[pl.ds(pl.multiple_of(there * 288, 32), 288), cols] = both.astype(BF16)

    c_copies = [between(k, c) for k in range(NX)]
    c_copies[0].start()
    for k, before in ((1, 0), (3, 1), (2, 3)):
        there = ((x - k) & (NX - 1))
        remote(slots.at[c, there], slots.at[c, there], x_send.at[k], x_recv.at[k], dev_x(k)).wait_recv()
        c_copies[k].start()
        between(before, 1 - c).wait_recv()
        spread_rows(before)
    between(2, 1 - c).wait_recv()
    spread_rows(2)

    def chunk(j):
        for k in (0,) + ORDER:
            there = at_z((NZ - k) % NZ)
            if k:
                remote(columns(there, j), got.at[j, there], z_send.at[j, k], z_recv.at[j, k], dev_z(k)).wait_recv()
            got[j, there] = got[j, there] * keep[pl.ds(there, 1), pl.ds(j * CW, CW)].astype(BF16)
        block = got[j].reshape(NAUX, CW)
        acc = jnp.zeros((1, CW), F32)
        for i in range(NAUX // QB):
            image = jnp.dot(dense[pl.ds(i * QB, QB), :], block, preferred_element_type=F32)
            acc = acc + jnp.sum(block[i * QB : (i + 1) * QB].astype(F32) * image, axis=0, keepdims=True)
        pieces = [acc[:, i * LANES : (i + 1) * LANES] for i in range(CW // LANES)]
        terms[j] = jnp.concatenate(pieces + [jnp.zeros((8 - len(pieces), LANES), F32)], axis=0)
        copies = [
            remote(terms.at[j], heard.at[j, c * NZ + z], t_send.at[j, int(flip), k], t_recv.at[j], dev_zc(k, flip))
            for k in ORDER + (0,) for flip in (False, True) if k or flip
        ]
        for copy in copies:
            copy.start()
        heard[j, c * NZ + z] = terms[j]
        return copies

    def owned(j):
        others = heard.at[j, pl.ds(0, 2 * NZ - 1)]
        pltpu.make_async_copy(others, others, t_recv.at[j]).wait()
        value = heard[j].reshape(192, LANES)
        first = value.astype(BF16)
        value = value - first.astype(F32)
        second = value.astype(BF16)
        third = (value - second.astype(F32)).astype(BF16)
        sums = [jnp.dot(hits[j], v, preferred_element_type=F32) for v in (third, second, first)]
        both = sums[0] + sums[1] + sums[2]
        return jnp.where(iota((32, LANES), 1) < 64, both[:32], both[32:])

    t_copies = [chunk(0)]
    total = None
    for j in range(1, CHUNKS):
        t_copies.append(chunk(j))
        mine = owned(j - 1)
        total = mine if total is None else total + mine
    for group in [y_copies, x_copies, c_copies, [o_copy], m_copies] + z_copies + t_copies:
        for copy in group:
            copy.wait_send()
    mine = owned(CHUNKS - 1)
    total = mine if total is None else total + mine

    for i in range(NX * NY):
        part[i] = total[i : i + 1]
    p_copies = [
        remote(part.at[place_at(k)], rows_in.at[place], p_send.at[i], p_recv, dev_xy(k)) for i, k in enumerate(AROUND)
    ]
    for copy in p_copies:
        copy.start()
    rows_in[place] = part[place]
    for copy in p_copies:
        copy.wait_send()
    others = rows_in.at[pl.ds(0, NX * NY - 1)]
    pltpu.make_async_copy(others, others, p_recv).wait()
    both = jnp.sum(rows_in[...], axis=0)
    out_ref[...] = both[:, :64] + both[:, 64:]


def body(integrals, tile_mask, metric, owners):
    any_spec = pl.BlockSpec(memory_space=pl.ANY)
    dma = pltpu.SemaphoreType.DMA
    return pl.pallas_call(
        kernel,
        out_shape=jax.ShapeDtypeStruct((1, 64), F32),
        in_specs=[any_spec] * 4,
        out_specs=pl.BlockSpec(memory_space=pltpu.VMEM),
        scratch_shapes=[
            pltpu.VMEM((CHUNKS, NZ, AUXD, CW), BF16),
            pltpu.VMEM((NZ, 1, 96), I32),
            pltpu.VMEM((16, WIDTH), F32),
            pltpu.VMEM((SHARD, NAUX), BF16),
            pltpu.VMEM((2, 1, 96), I32),
            pltpu.VMEM((2, NX, NY, MAIN, PACKED), BF16),
            pltpu.VMEM((NAUX, NAUX), BF16),
            pltpu.VMEM((CHUNKS, 64, 192), BF16),
            pltpu.VMEM((CHUNKS, 8, LANES), F32),
            pltpu.VMEM((CHUNKS, 2 * NZ, 8, LANES), F32),
            pltpu.VMEM((NX * NY, 1, LANES), F32),
            pltpu.VMEM((NX * NY, 1, LANES), F32),
            dma((3 + CHUNKS,)),
            dma((CHUNKS, NZ)), dma((CHUNKS, NZ)),
            dma((NZ,)), dma((NZ,)),
            dma, dma,
            dma((NY,)), dma((NY,)),
            dma((NX,)), dma((NX,)),
            dma((NX,)), dma((NX,)),
            dma((CHUNKS, 2, NZ)), dma((CHUNKS,)),
            dma((NX * NY,)), dma,
        ],
        compiler_params=pltpu.CompilerParams(collective_id=0, has_side_effects=True),
    )(integrals, tile_mask, metric, owners.reshape(1, -1))


def solution(mesh):
    return jax.shard_map(
        body,
        mesh=mesh,
        in_specs=(P("aux", "pair"), P("aux", "pair"), P("pair", None), P("pair")),
        out_specs=P(("aux", "pair"), None),
        check_vma=False,
    )
```
